1024 devices in a mesh: row: 8 (over z_hi, core), col: 128 (over y, x, z_lo).
Axes of the slice: x: 4, y: 4, z: 32 (z_hi: 4, z_lo: 8; z = z_hi * 8 + z_lo), core: 2. Of those that a mesh axis runs over, the one named last changes fastest.
Arguments:
- strip_factors: bfloat16 [32768, 64], P(('row', 'col')), may hold values from -8 to 8
- sku_factors: bfloat16 [262144, 64], P('col', 'row'), may hold values from -8 to 8
- probe: bfloat16 [262144, 16], P('col', 'row'), may hold values from -6 to 6
- demand_weight: float32 [1, 32768], P(None, ('row', 'col')), may hold values from 1 to 30, as said below
Outputs:
- basis: float32 [16, 32768], P(None, ('row', 'col'))
The draws below stay inside these ranges and needn't reach their ends.
Inputs may be any that keep to these rules, and one draw needn't show every extreme that they name: `demand_weight`: positive weights.
All inputs are finite; a program needn't handle non-finite values.
Results may differ from the reference program's by a relative error of at most 0.009.
The reference program's roundings to bfloat16 on the way (of `strip_unit`, `sku_unit` and `affinity`) count: a program that leaves them out, or rounds other values in their place, can miss the bound.
Values may be sent and summed in bfloat16 or wider, within the bound.
No kernel may reach another device: no remote copies, remote signals or barrier semaphores. Data moves between devices by JAX's collectives and lax.ppermute only.
A program may use at most 32 MiB of HBM per device.

```python
import jax
import jax.numpy as jnp
from jax import lax

K = 64
BLOCK = 16
C_BLK = 2048
STRIP = 32768
SKUS = 262144
N_COL = 128


cluster_count = 32


root_count = 4


def cluster_centres(key):
    root_rows = jnp.clip(jax.random.normal(jax.random.fold_in(key, 101), (root_count, K), jnp.float32), -4.0, 4.0)
    own_rows = jnp.clip(jax.random.normal(jax.random.fold_in(key, 102), (cluster_count, K), jnp.float32), -4.0, 4.0)
    parent = jnp.arange(cluster_count) % root_count
    return 0.8 * root_rows[parent] + 0.6 * own_rows


def member_rows(centres, key, jitter, spread_low, spread_high):
    row_count = jitter.shape[0]
    member_ids = jax.random.randint(jax.random.fold_in(key, 1), (row_count,), 0, cluster_count)
    sign_flip = (jax.random.randint(jax.random.fold_in(key, 2), (row_count, 1), 0, 2) * 2 - 1).astype(jnp.float32)
    spread = jnp.exp(jax.random.uniform(jax.random.fold_in(key, 3), (row_count, 1), jnp.float32, jnp.log(spread_low), jnp.log(spread_high)))
    return sign_flip * centres[member_ids] + spread * jitter


def draw_strip_factors(key, part):
    centres = cluster_centres(key)
    key = jax.random.fold_in(key, 5)
    jitter_key = jax.random.fold_in(key, 4)
    jitter = jnp.clip(jax.random.normal(jitter_key, (STRIP, K), jnp.float32), -4.0, 4.0)
    rows = member_rows(centres, key, jitter, 0.15, 0.6)
    return rows.astype(jnp.bfloat16)


def draw_sku_factors(key, part):
    centres = cluster_centres(key)
    key = jax.random.fold_in(key, 7)
    jitter_key = jax.random.fold_in(key, 4)
    jitter = jnp.clip(jax.random.normal(jitter_key, (SKUS, K), jnp.float32), -4.0, 4.0)
    rows = member_rows(centres, key, jitter, 0.15, 0.6)
    return rows.astype(jnp.bfloat16)


def draw_demand_weight(key, part):
    key = jax.random.fold_in(key, 11)
    place = jnp.arange(STRIP, dtype=jnp.float32) / STRIP
    ramp = jnp.exp(place * jnp.log(3.0))
    base = jnp.exp(jax.random.uniform(key, (1, STRIP), jnp.float32, 0.0, jnp.log(10.0)))
    return (base * ramp).astype(jnp.float32)


def block_scale(key, shape, shards, smallest, top_value):
    loudness, own = 1.0, jax.random.fold_in(key, 6)
    for dim, shards_of in shards:
        steps = jnp.exp(jax.random.uniform(jax.random.fold_in(own, dim), (shards_of,), jnp.float32, smallest / len(shards), top_value / len(shards)))
        loudness = loudness * jnp.repeat(steps, shape[dim] // shards_of).reshape([-1 if axis == dim else 1 for axis in range(len(shape))])
    return loudness


def bell_draw(key, dims, scale, most, pieces=(), kind=jnp.bfloat16):
    array = scale * jax.random.normal(key, dims, jnp.float32)
    if pieces:
        array = array * block_scale(key, dims, pieces, -0.22, 0.18)
    return jnp.clip(array, -most, most).astype(kind)


def setup_inputs(seed: int = 0) -> dict:
    splits = jax.random.split(jax.random.key(seed), 5)
    return {
        "strip_factors": draw_strip_factors(jax.random.fold_in(splits[4], 71), 0),
        "sku_factors": draw_sku_factors(jax.random.fold_in(splits[4], 71), 0),
        "probe": bell_draw(splits[2], (SKUS, BLOCK), 1.0, 6.0, ((0, 128), (1, 8))),
        "demand_weight": draw_demand_weight(jax.random.fold_in(splits[4], 71), 0),
    }


def unit_rows(factors):
    wide = factors.astype(jnp.float32)
    scale = lax.rsqrt(lax.optimization_barrier(jnp.sum(wide * wide, axis=1, keepdims=True)) + 1e-06)
    return (wide * scale).astype(jnp.bfloat16)

def reference(strip_factors, sku_factors, probe, demand_weight):
    strip_unit = unit_rows(strip_factors)
    sku_unit = unit_rows(sku_factors)
    panels = sku_unit.reshape(N_COL, C_BLK, K)
    probes = probe.reshape(N_COL, C_BLK, BLOCK)

    def add_block(total, pair):
        panel, columns = pair
        corr = jnp.dot(strip_unit.astype(jnp.float32), panel.T.astype(jnp.float32), preferred_element_type=jnp.float32)
        affinity = jnp.exp(corr).astype(jnp.bfloat16)
        return (total + jnp.dot(affinity.astype(jnp.float32), columns.astype(jnp.float32), preferred_element_type=jnp.float32).T, None)
    start = jnp.zeros((BLOCK, STRIP), jnp.float32)
    image, unused = lax.scan(add_block, start, (panels, probes))
    gram = jnp.dot(image * demand_weight, image.T, precision=lax.Precision.HIGHEST)
    lower = jnp.linalg.cholesky(gram)
    return jax.scipy.linalg.solve_triangular(lower, image, lower=True)
```

```python
import jax
import jax.numpy as jnp
from jax import lax
from jax.experimental import pallas as pl
from jax.experimental.pallas import tpu as pltpu
from jax.sharding import Mesh
from jax.sharding import PartitionSpec as P

F32, BF16 = jnp.float32, jnp.bfloat16
AXES = ("z_hi", "core", "y", "x", "z_lo")
SIZES = (4, 2, 4, 4, 8)
ROW, COL = ("z_hi", "core"), ("y", "x", "z_lo")
VMEM = pl.BlockSpec(memory_space=pltpu.VMEM)
SMEM = pl.BlockSpec(memory_space=pltpu.SMEM)
T_STEP, S_STEP = 1024, 256


def kernel_call(body, outs, count, scratch=(), smem=0, name=None, **cost):
    return pl.pallas_call(
        body,
        out_shape=outs,
        in_specs=[SMEM] * smem + [VMEM] * (count - smem),
        out_specs=jax.tree.map(lambda _: VMEM, outs),
        scratch_shapes=list(scratch),
        name=name,
        compiler_params=pltpu.CompilerParams(vmem_limit_bytes=40 * 2**20),
    )


def shape(dims, kind=F32):
    return jax.ShapeDtypeStruct(dims, kind)


def pack_kernel(strip_ref, sku_ref, probe_ref, strips_ref, skus_ref):
    wide = strip_ref[...].astype(F32)
    scale = lax.rsqrt(jnp.sum(wide * wide, axis=1, keepdims=True) + 1e-06)
    unit = wide * scale
    packed = jnp.concatenate([unit[:16], unit[16:]], axis=1).astype(BF16)
    strips_ref[...] = jnp.broadcast_to(packed[None], strips_ref.shape)
    sku = sku_ref[...].astype(F32)
    probe = probe_ref[...].astype(F32)
    factors = jnp.concatenate([sku[:, :1024], sku[:, 1024:]], axis=0)
    columns = jnp.concatenate([probe[:, 256 * m : 256 * (m + 1)] for m in range(8)], axis=0)
    skus_ref[...] = jnp.concatenate([factors, columns], axis=1).astype(BF16)


def image_kernel(z_hi_ref, strips_ref, panel_ref, out_ref, wide_ref, columns_ref, unit_ref, turned_ref):
    z_hi = z_hi_ref[0]
    for back in range(4):
        place = lax.rem(z_hi + 4 - back, 4)
        for core in range(2):
            piece = panel_ref[core, back].astype(F32)
            wide_ref[place, core, :, :1024] = piece[:8, :1024]
            wide_ref[place, core, :, 1024:] = piece[8:, :1024]
            for m in range(8):
                columns_ref[place, core, :, 256 * m : 256 * (m + 1)] = piece[2 * m : 2 * m + 2, 1024:]
    wide = wide_ref[...].reshape(64, 2048)
    scale = lax.rsqrt(jnp.sum(wide * wide, axis=0, keepdims=True) + 1e-06)
    unit_ref[...] = (wide * scale).astype(BF16).T
    probe = jnp.concatenate([columns_ref[r // 2, r % 2] for r in range(8)], axis=0).astype(BF16)
    turned_ref[...] = strips_ref[...].T
    for half in range(2):
        for step in range(2048 // T_STEP):
            strip = turned_ref[64 * half : 64 * half + 64, T_STEP * step : T_STEP * (step + 1)]
            total = jnp.zeros((16, T_STEP), F32)
            for number in range(2048 // S_STEP):
                skus = slice(number * S_STEP, (number + 1) * S_STEP)
                corr = jnp.dot(unit_ref[skus, :], strip, preferred_element_type=F32)
                affinity = jnp.exp(corr).astype(BF16)
                total = total + jnp.dot(probe[:, skus], affinity, preferred_element_type=F32)
            for k in range(T_STEP // 128):
                out_ref[step * (T_STEP // 128) + k, 16 * half : 16 * half + 16, :] = total[:, 128 * k : 128 * (k + 1)]


def turn_kernel(parts_ref, out_ref):
    total = parts_ref[0]
    for k in range(1, parts_ref.shape[0]):
        total = total + parts_ref[k]
    turned = total.T.reshape(8, 16, 32)
    out_ref[...] = jnp.concatenate([turned[:, 4 * b : 4 * b + 4, :] for b in range(4)], axis=2)


def gram_kernel(parts_ref, weight_ref, image_ref, gram_ref):
    total = parts_ref[0]
    for k in range(1, parts_ref.shape[0]):
        total = total + parts_ref[k]
    turned = jnp.concatenate([total[:, 32 * b : 32 * b + 32] for b in range(4)], axis=0).T
    image = jnp.concatenate([turned[:16], turned[16:]], axis=1)
    image_ref[...] = image
    gram = lax.dot_general(
        image * weight_ref[...], image, (((1,), (1,)), ((), ())),
        precision=lax.Precision.HIGHEST, preferred_element_type=F32,
    )
    packed = jnp.concatenate([gram[:8], gram[8:], jnp.zeros((8, 96), F32)], axis=1)
    gram_ref[...] = jnp.broadcast_to(packed[None], gram_ref.shape)


def sum_kernel(parts_ref, out_ref):
    total = parts_ref[0]
    for k in range(1, parts_ref.shape[0]):
        total = total + parts_ref[k]
    out_ref[...] = jnp.broadcast_to(total[None], out_ref.shape)


def basis_kernel(parts_ref, image_ref, out_ref):
    total = parts_ref[0]
    for k in range(1, parts_ref.shape[0]):
        total = total + parts_ref[k]
    gram = jnp.concatenate([total[:, :16], total[:, 16:32]], axis=0)
    left = image_ref[...]
    rows = lax.broadcasted_iota(jnp.int32, (16, 1), 0)
    for k in range(15):
        below = rows > k
        ratio = jnp.where(below, gram[:, k : k + 1] / gram[k : k + 1, k : k + 1], 0.0)
        left = left - ratio * left[k : k + 1, :]
        gram = gram - ratio * gram[k : k + 1, :]
    diagonal = rows == lax.broadcasted_iota(jnp.int32, (16, 16), 1)
    pivots = jnp.sum(jnp.where(diagonal, gram, 0.0), axis=1, keepdims=True)
    out_ref[...] = left / jnp.sqrt(pivots)


def per_device(strip_factors, sku_factors, probe, demand_weight):
    strips, skus = kernel_call(
        pack_kernel, (shape((8, 16, 128), BF16), shape((16, 1280), BF16)), 3, name="pack"
    )(strip_factors, sku_factors.T, probe.T)
    shards = [skus] + [
        lax.ppermute(skus, "z_hi", [(i, (i + k) % 4) for i in range(4)]) for k in range(1, 4)
    ]
    strips = lax.all_to_all(strips, "z_lo", 0, 0, tiled=True).reshape(128, 128)
    strips = jnp.broadcast_to(strips[None], (16, 128, 128))
    strips = lax.all_to_all(strips, ("y", "x"), 0, 0, tiled=True).reshape(2048, 128)
    strips, *shards = lax.optimization_barrier((strips, *shards))
    panel = lax.all_gather(jnp.stack(shards), "core", axis=0)
    place = jnp.full((1,), lax.axis_index("z_hi"), jnp.int32)
    total = kernel_call(
        image_kernel, shape((16, 32, 128)), 3, smem=1, name="image",
        scratch=[pltpu.VMEM((4, 2, 8, 2048), F32), pltpu.VMEM((4, 2, 2, 2048), F32),
                 pltpu.VMEM((2048, 64), BF16), pltpu.VMEM((128, 2048), BF16)],
    )(place, strips, panel)
    total = lax.all_to_all(total, ("y", "x"), 0, 0, tiled=True)
    total = kernel_call(turn_kernel, shape((8, 4, 128)), 1, name="turn")(total)
    total = lax.all_to_all(total, "z_lo", 0, 0, tiled=True)
    image, gram = kernel_call(
        gram_kernel, (shape((16, 32)), shape((32, 8, 128))), 2, name="gram"
    )(total, demand_weight)
    gram = lax.all_to_all(gram, ("core", "y", "x"), 0, 0, tiled=True)
    gram = kernel_call(sum_kernel, shape((32, 8, 128)), 1, name="sum")(gram)
    gram = lax.all_to_all(gram, ("z_hi", "z_lo"), 0, 0, tiled=True)
    return kernel_call(basis_kernel, shape((16, 32)), 2, name="basis")(gram, image)


def solution(mesh):
    fine = Mesh(mesh.devices.reshape(SIZES), AXES)
    both = ROW + COL
    placed = (P(both, None), P(COL, ROW), P(COL, ROW), P(None, both))
    return jax.shard_map(
        per_device, mesh=fine, in_specs=placed, out_specs=P(None, both), check_vma=False
    )
```

```python
import jax
import jax.numpy as jnp
from jax import lax
from jax.experimental import pallas as pl
from jax.experimental.pallas import tpu as pltpu
from jax.sharding import Mesh
from jax.sharding import PartitionSpec as P

F32, BF16 = jnp.float32, jnp.bfloat16
AXES = ("z_hi", "core", "y", "x", "z_lo")
SIZES = (4, 2, 4, 4, 8)
ROW, COL = ("z_hi", "core"), ("y", "x", "z_lo")
VMEM = pl.BlockSpec(memory_space=pltpu.VMEM)
T_STEP, S_STEP = 1024, 256


def kernel_call(body, outs, count, scratch=(), name=None):
    return pl.pallas_call(
        body,
        out_shape=outs,
        in_specs=[VMEM] * count,
        out_specs=jax.tree.map(lambda _: VMEM, outs),
        scratch_shapes=list(scratch),
        name=name,
        compiler_params=pltpu.CompilerParams(vmem_limit_bytes=40 * 2**20),
    )


def shape(dims, kind=F32):
    return jax.ShapeDtypeStruct(dims, kind)


def pack_kernel(strip_ref, sku_ref, probe_ref, strips_ref, skus_ref):
    wide = strip_ref[...].astype(F32)
    scale = lax.rsqrt(jnp.sum(wide * wide, axis=1, keepdims=True) + 1e-06)
    unit = wide * scale
    packed = jnp.concatenate([unit[:16], unit[16:]], axis=1).astype(BF16)
    strips_ref[...] = jnp.broadcast_to(packed[None], strips_ref.shape)
    sku = sku_ref[...].astype(F32)
    probe = probe_ref[...].astype(F32)
    factors = jnp.concatenate([sku[:, :1024], sku[:, 1024:]], axis=0)
    columns = jnp.concatenate([probe[:, 256 * m : 256 * (m + 1)] for m in range(8)], axis=0)
    skus_ref[...] = jnp.concatenate([factors, columns], axis=1).astype(BF16)


def image_kernel(strips_ref, panel_ref, out_ref, wide_ref, columns_ref, unit_ref, turned_ref):
    for place in range(4):
        for core in range(2):
            piece = panel_ref[core, place].astype(F32)
            wide_ref[place, core, :, :1024] = piece[:8, :1024]
            wide_ref[place, core, :, 1024:] = piece[8:, :1024]
            for m in range(8):
                columns_ref[place, core, :, 256 * m : 256 * (m + 1)] = piece[2 * m : 2 * m + 2, 1024:]
    wide = wide_ref[...].reshape(64, 2048)
    scale = lax.rsqrt(jnp.sum(wide * wide, axis=0, keepdims=True) + 1e-06)
    unit_ref[...] = (wide * scale).astype(BF16).T
    probe = jnp.concatenate([columns_ref[r // 2, r % 2] for r in range(8)], axis=0).astype(BF16)
    turned_ref[...] = strips_ref[...].T
    for half in range(2):
        for step in range(2048 // T_STEP):
            strip = turned_ref[64 * half : 64 * half + 64, T_STEP * step : T_STEP * (step + 1)]
            total = jnp.zeros((16, T_STEP), F32)
            for number in range(2048 // S_STEP):
                skus = slice(number * S_STEP, (number + 1) * S_STEP)
                corr = jnp.dot(unit_ref[skus, :], strip, preferred_element_type=F32)
                affinity = jnp.exp(corr).astype(BF16)
                total = total + jnp.dot(probe[:, skus], affinity, preferred_element_type=F32)
            for k in range(T_STEP // 128):
                out_ref[step * (T_STEP // 128) + k, 16 * half : 16 * half + 16, :] = total[:, 128 * k : 128 * (k + 1)]


def turn_kernel(parts_ref, out_ref):
    total = parts_ref[0]
    for k in range(1, parts_ref.shape[0]):
        total = total + parts_ref[k]
    turned = total.T.reshape(8, 16, 32)
    out_ref[...] = jnp.concatenate([turned[:, 4 * b : 4 * b + 4, :] for b in range(4)], axis=2)


def gram_kernel(parts_ref, weight_ref, image_ref, gram_ref):
    total = parts_ref[0]
    for k in range(1, parts_ref.shape[0]):
        total = total + parts_ref[k]
    turned = jnp.concatenate([total[:, 32 * b : 32 * b + 32] for b in range(4)], axis=0).T
    image = jnp.concatenate([turned[:16], turned[16:]], axis=1)
    image_ref[...] = image
    gram = lax.dot_general(
        image * weight_ref[...], image, (((1,), (1,)), ((), ())),
        precision=lax.Precision.HIGHEST, preferred_element_type=F32,
    )
    packed = jnp.concatenate([gram[2 * b : 2 * b + 2] for b in range(8)], axis=1)
    gram_ref[...] = jnp.broadcast_to(packed[None], gram_ref.shape)


def sum_kernel(parts_ref, out_ref):
    total = parts_ref[0]
    for k in range(1, parts_ref.shape[0]):
        total = total + parts_ref[k]
    out_ref[...] = jnp.broadcast_to(total[None], out_ref.shape)


def basis_kernel(parts_ref, image_ref, out_ref):
    total = parts_ref[0]
    for k in range(1, parts_ref.shape[0]):
        total = total + parts_ref[k]
    gram = jnp.concatenate([total[:, 16 * b : 16 * b + 16] for b in range(8)], axis=0)
    left = image_ref[...]
    rows = lax.broadcasted_iota(jnp.int32, (16, 1), 0)
    for k in range(15):
        below = rows > k
        ratio = jnp.where(below, gram[:, k : k + 1] / gram[k : k + 1, k : k + 1], 0.0)
        left = left - ratio * left[k : k + 1, :]
        gram = gram - ratio * gram[k : k + 1, :]
    diagonal = rows == lax.broadcasted_iota(jnp.int32, (16, 16), 1)
    pivots = jnp.sum(jnp.where(diagonal, gram, 0.0), axis=1, keepdims=True)
    out_ref[...] = left / jnp.sqrt(pivots)


def per_device(strip_factors, sku_factors, probe, demand_weight):
    strips, skus = kernel_call(
        pack_kernel, (shape((128, 16, 128), BF16), shape((16, 1280), BF16)), 3, name="pack"
    )(strip_factors, sku_factors.T, probe.T)
    panel = lax.all_gather(skus, "z_hi", axis=0)
    strips = lax.all_to_all(strips, COL, 0, 0, tiled=True).reshape(2048, 128)
    panel = lax.all_gather(panel, "core", axis=0)
    total = kernel_call(
        image_kernel, shape((16, 32, 128)), 2, name="image",
        scratch=[pltpu.VMEM((4, 2, 8, 2048), F32), pltpu.VMEM((4, 2, 2, 2048), F32),
                 pltpu.VMEM((2048, 64), BF16), pltpu.VMEM((128, 2048), BF16)],
    )(strips, panel)
    total = lax.all_to_all(total, ("y", "x"), 0, 0, tiled=True)
    total = kernel_call(turn_kernel, shape((8, 4, 128)), 1, name="turn")(total)
    total = lax.all_to_all(total, "z_lo", 0, 0, tiled=True)
    image, gram = kernel_call(
        gram_kernel, (shape((16, 32)), shape((32, 2, 128))), 2, name="gram"
    )(total, demand_weight)
    gram = lax.all_to_all(gram, ("core", "y", "x"), 0, 0, tiled=True)
    gram = kernel_call(sum_kernel, shape((32, 2, 128)), 1, name="sum")(gram)
    gram = lax.all_to_all(gram, ("z_hi", "z_lo"), 0, 0, tiled=True)
    return kernel_call(basis_kernel, shape((16, 32)), 2, name="basis")(gram, image)


def solution(mesh):
    fine = Mesh(mesh.devices.reshape(SIZES), AXES)
    both = ROW + COL
    placed = (P(both, None), P(COL, ROW), P(COL, ROW), P(None, both))
    return jax.shard_map(
        per_device, mesh=fine, in_specs=placed, out_specs=P(None, both), check_vma=False
    )
```

```python
import jax
import jax.numpy as jnp
from jax import lax
from jax.experimental import pallas as pl
from jax.experimental.pallas import tpu as pltpu
from jax.sharding import Mesh
from jax.sharding import PartitionSpec as P

F32, BF16 = jnp.float32, jnp.bfloat16
AXES = ("z_hi", "core", "y", "x", "z_lo")
SIZES = (4, 2, 4, 4, 8)
ROW, COL = ("z_hi", "core"), ("y", "x", "z_lo")
VMEM = pl.BlockSpec(memory_space=pltpu.VMEM)
T_STEP, S_STEP = 1024, 512


def kernel_call(body, outs, count, scratch=(), name=None, room=40):
    return pl.pallas_call(
        body,
        out_shape=outs,
        in_specs=[VMEM] * count,
        out_specs=jax.tree.map(lambda _: VMEM, outs),
        scratch_shapes=list(scratch),
        name=name,
        compiler_params=pltpu.CompilerParams(vmem_limit_bytes=room * 2**20),
    )


def shape(dims, kind=F32):
    return jax.ShapeDtypeStruct(dims, kind)


def pack_kernel(strip_ref, sku_ref, probe_ref, strips_ref, skus_ref):
    wide = strip_ref[...].astype(F32)
    scale = lax.rsqrt(jnp.sum(wide * wide, axis=1, keepdims=True) + 1e-06)
    unit = wide * scale
    packed = jnp.concatenate([unit[:16], unit[16:]], axis=1).astype(BF16)
    strips_ref[...] = jnp.broadcast_to(packed[None], strips_ref.shape)
    sku = sku_ref[...].astype(F32)
    probe = probe_ref[...].astype(F32)
    factors = jnp.concatenate([sku[:, :1024], sku[:, 1024:]], axis=0)
    columns = jnp.concatenate([probe[:, 256 * m : 256 * (m + 1)] for m in range(8)], axis=0)
    skus_ref[...] = jnp.concatenate([factors, columns], axis=1).astype(BF16)


def prepare_kernel(panel_ref, unit_ref, probe_ref):
    factors, columns = [], []
    for z_hi in range(4):
        for core in range(2):
            piece = panel_ref[core, z_hi].astype(F32)
            factors.append(jnp.concatenate([piece[:8, :1024], piece[8:, :1024]], axis=1))
            columns.append(jnp.concatenate([piece[2 * m : 2 * m + 2, 1024:] for m in range(8)], axis=1))
    wide = jnp.concatenate(factors, axis=0)
    scale = lax.rsqrt(jnp.sum(wide * wide, axis=0, keepdims=True) + 1e-06)
    unit_ref[...] = (wide * scale).astype(BF16).T
    probe_ref[...] = jnp.concatenate(columns, axis=0).astype(BF16)


def image_kernel(strips_ref, unit_ref, probe_ref, out_ref, turned_ref):
    turned_ref[...] = strips_ref[...].T
    for half in range(2):
        for step in range(2048 // T_STEP):
            strip = turned_ref[64 * half : 64 * half + 64, T_STEP * step : T_STEP * (step + 1)]
            total = jnp.zeros((16, T_STEP), F32)
            for number in range(2048 // S_STEP):
                skus = slice(number * S_STEP, (number + 1) * S_STEP)
                corr = jnp.dot(unit_ref[skus, :], strip, preferred_element_type=F32)
                affinity = jnp.exp(corr).astype(BF16)
                total = total + jnp.dot(probe_ref[:, skus], affinity, preferred_element_type=F32)
            for k in range(T_STEP // 128):
                out_ref[step * (T_STEP // 128) + k, 16 * half : 16 * half + 16, :] = total[:, 128 * k : 128 * (k + 1)]


def turn_kernel(parts_ref, out_ref):
    total = parts_ref[0]
    for k in range(1, parts_ref.shape[0]):
        total = total + parts_ref[k]
    turned = total.T.reshape(8, 16, 32)
    out_ref[...] = jnp.concatenate([turned[:, 4 * b : 4 * b + 4, :] for b in range(4)], axis=2)


def gram_kernel(parts_ref, weight_ref, image_ref, gram_ref):
    total = parts_ref[0]
    for k in range(1, parts_ref.shape[0]):
        total = total + parts_ref[k]
    turned = jnp.concatenate([total[:, 32 * b : 32 * b + 32] for b in range(4)], axis=0).T
    image = jnp.concatenate([turned[:16], turned[16:]], axis=1)
    image_ref[...] = image
    gram = lax.dot_general(
        image * weight_ref[...], image, (((1,), (1,)), ((), ())),
        precision=lax.Precision.HIGHEST, preferred_element_type=F32,
    )
    packed = jnp.concatenate([gram[2 * b : 2 * b + 2] for b in range(8)], axis=1)
    gram_ref[...] = jnp.broadcast_to(packed[None], gram_ref.shape)


def sum_kernel(parts_ref, out_ref):
    total = parts_ref[0]
    for k in range(1, parts_ref.shape[0]):
        total = total + parts_ref[k]
    out_ref[...] = jnp.broadcast_to(total[None], out_ref.shape)


def basis_kernel(parts_ref, image_ref, out_ref):
    total = parts_ref[0]
    for k in range(1, parts_ref.shape[0]):
        total = total + parts_ref[k]
    gram = jnp.concatenate([total[:, 16 * b : 16 * b + 16] for b in range(8)], axis=0)
    left = image_ref[...]
    rows = lax.broadcasted_iota(jnp.int32, (16, 1), 0)
    for k in range(15):
        below = rows > k
        ratio = jnp.where(below, gram[:, k : k + 1] / gram[k : k + 1, k : k + 1], 0.0)
        left = left - ratio * left[k : k + 1, :]
        gram = gram - ratio * gram[k : k + 1, :]
    diagonal = rows == lax.broadcasted_iota(jnp.int32, (16, 16), 1)
    pivots = jnp.sum(jnp.where(diagonal, gram, 0.0), axis=1, keepdims=True)
    out_ref[...] = left / jnp.sqrt(pivots)


def per_device(strip_factors, sku_factors, probe, demand_weight):
    strips, skus = kernel_call(
        pack_kernel, (shape((8, 16, 128), BF16), shape((16, 1280), BF16)), 3, name="pack", room=63
    )(strip_factors, sku_factors.T, probe.T)
    panel = lax.all_gather(skus, "z_hi", axis=0)
    strips = lax.all_to_all(strips, "z_lo", 0, 0, tiled=True).reshape(128, 128)
    strips, panel = lax.optimization_barrier((strips, panel))
    strips = jnp.broadcast_to(strips[None], (16, 128, 128))
    strips = lax.all_to_all(strips, ("y", "x"), 0, 0, tiled=True).reshape(2048, 128)
    panel = lax.all_gather(panel, "core", axis=0)
    unit, columns = kernel_call(
        prepare_kernel, (shape((2048, 64), BF16), shape((16, 2048), BF16)), 1, name="prepare"
    )(panel)
    total = kernel_call(
        image_kernel, shape((16, 32, 128)), 3, name="image", scratch=[pltpu.VMEM((128, 2048), BF16)]
    )(strips, unit, columns)
    total = lax.all_to_all(total, ("y", "x"), 0, 0, tiled=True)
    total = kernel_call(turn_kernel, shape((8, 4, 128)), 1, name="turn")(total)
    total = lax.all_to_all(total, "z_lo", 0, 0, tiled=True)
    image, gram = kernel_call(
        gram_kernel, (shape((16, 32)), shape((32, 2, 128))), 2, name="gram"
    )(total, demand_weight)
    gram = lax.all_to_all(gram, ("core", "y", "x"), 0, 0, tiled=True)
    gram = kernel_call(sum_kernel, shape((32, 2, 128)), 1, name="sum")(gram)
    gram = lax.all_to_all(gram, ("z_hi", "z_lo"), 0, 0, tiled=True)
    return kernel_call(basis_kernel, shape((16, 32)), 2, name="basis")(gram, image)


def solution(mesh):
    fine = Mesh(mesh.devices.reshape(SIZES), AXES)
    both = ROW + COL
    placed = (P(both, None), P(COL, ROW), P(COL, ROW), P(None, both))
    return jax.shard_map(
        per_device, mesh=fine, in_specs=placed, out_specs=P(None, both), check_vma=False
    )
```

```python
import jax
import jax.numpy as jnp
from jax import lax
from jax.experimental import pallas as pl
from jax.experimental.pallas import tpu as pltpu
from jax.sharding import Mesh
from jax.sharding import PartitionSpec as P

F32, BF16 = jnp.float32, jnp.bfloat16
AXES = ("z_hi", "core", "y", "x", "z_lo")
SIZES = (4, 2, 4, 4, 8)
ROW, COL = ("z_hi", "core"), ("y", "x", "z_lo")
VMEM = pl.BlockSpec(memory_space=pltpu.VMEM)
T_STEP, S_STEP = 1024, 512


def kernel_call(body, outs, count, scratch=(), name=None, room=40):
    return pl.pallas_call(
        body,
        out_shape=outs,
        in_specs=[VMEM] * count,
        out_specs=jax.tree.map(lambda _: VMEM, outs),
        scratch_shapes=list(scratch),
        name=name,
        compiler_params=pltpu.CompilerParams(vmem_limit_bytes=room * 2**20),
    )


def shape(dims, kind=F32):
    return jax.ShapeDtypeStruct(dims, kind)


def pack_kernel(strip_ref, sku_ref, probe_ref, strips_ref, skus_ref):
    wide = strip_ref[...].astype(F32)
    scale = lax.rsqrt(jnp.sum(wide * wide, axis=1, keepdims=True) + 1e-06)
    unit = wide * scale
    packed = jnp.concatenate([unit[:16], unit[16:]], axis=1).astype(BF16)
    strips_ref[...] = jnp.broadcast_to(packed[None], strips_ref.shape)
    sku = sku_ref[...].astype(F32)
    probe = probe_ref[...].astype(F32)
    factors = jnp.concatenate([sku[:, :1024], sku[:, 1024:]], axis=0)
    columns = jnp.concatenate([probe[:, 256 * m : 256 * (m + 1)] for m in range(8)], axis=0)
    skus_ref[...] = jnp.concatenate([factors, columns], axis=1).astype(BF16)


def prepare_kernel(panel_ref, unit_ref, probe_ref):
    factors, columns = [], []
    for z_hi in range(4):
        for core in range(2):
            piece = panel_ref[core, z_hi].astype(F32)
            factors.append(jnp.concatenate([piece[:8, :1024], piece[8:, :1024]], axis=1))
            columns.append(jnp.concatenate([piece[2 * m : 2 * m + 2, 1024:] for m in range(8)], axis=1))
    wide = jnp.concatenate(factors, axis=0)
    scale = lax.rsqrt(jnp.sum(wide * wide, axis=0, keepdims=True) + 1e-06)
    unit_ref[...] = (wide * scale).astype(BF16).T
    probe_ref[...] = jnp.concatenate(columns, axis=0).astype(BF16)


def image_kernel(strips_ref, unit_ref, probe_ref, out_ref, turned_ref):
    turned_ref[...] = strips_ref[...].T
    for half in range(2):
        for step in range(2048 // T_STEP):
            strip = turned_ref[64 * half : 64 * half + 64, T_STEP * step : T_STEP * (step + 1)]
            total = jnp.zeros((16, T_STEP), F32)
            for number in range(2048 // S_STEP):
                skus = slice(number * S_STEP, (number + 1) * S_STEP)
                corr = jnp.dot(unit_ref[skus, :], strip, preferred_element_type=F32)
                affinity = jnp.exp(corr).astype(BF16)
                total = total + jnp.dot(probe_ref[:, skus], affinity, preferred_element_type=F32)
            for k in range(T_STEP // 128):
                out_ref[step * (T_STEP // 128) + k, 16 * half : 16 * half + 16, :] = total[:, 128 * k : 128 * (k + 1)]


def turn_kernel(parts_ref, out_ref):
    total = parts_ref[0]
    for k in range(1, parts_ref.shape[0]):
        total = total + parts_ref[k]
    turned = total.T.reshape(8, 16, 32)
    out_ref[...] = jnp.concatenate([turned[:, 4 * b : 4 * b + 4, :] for b in range(4)], axis=2)


def gram_kernel(parts_ref, weight_ref, image_ref, gram_ref):
    total = parts_ref[0]
    for k in range(1, parts_ref.shape[0]):
        total = total + parts_ref[k]
    turned = jnp.concatenate([total[:, 32 * b : 32 * b + 32] for b in range(4)], axis=0).T
    image = jnp.concatenate([turned[:16], turned[16:]], axis=1)
    image_ref[...] = image
    gram = lax.dot_general(
        image * weight_ref[...], image, (((1,), (1,)), ((), ())),
        precision=lax.Precision.HIGHEST, preferred_element_type=F32,
    )
    packed = jnp.concatenate([gram[2 * b : 2 * b + 2] for b in range(8)], axis=1)
    gram_ref[...] = jnp.broadcast_to(packed[None], gram_ref.shape)


def sum_kernel(parts_ref, out_ref):
    total = parts_ref[0]
    for k in range(1, parts_ref.shape[0]):
        total = total + parts_ref[k]
    out_ref[...] = jnp.broadcast_to(total[None], out_ref.shape)


def basis_kernel(parts_ref, image_ref, out_ref):
    total = parts_ref[0]
    for k in range(1, parts_ref.shape[0]):
        total = total + parts_ref[k]
    gram = jnp.concatenate([total[:, 16 * b : 16 * b + 16] for b in range(8)], axis=0)
    left = image_ref[...]
    rows = lax.broadcasted_iota(jnp.int32, (16, 1), 0)
    for k in range(15):
        below = rows > k
        ratio = jnp.where(below, gram[:, k : k + 1] / gram[k : k + 1, k : k + 1], 0.0)
        left = left - ratio * left[k : k + 1, :]
        gram = gram - ratio * gram[k : k + 1, :]
    diagonal = rows == lax.broadcasted_iota(jnp.int32, (16, 16), 1)
    pivots = jnp.sum(jnp.where(diagonal, gram, 0.0), axis=1, keepdims=True)
    out_ref[...] = left / jnp.sqrt(pivots)


def from_first(pieces, axes, first):
    others = [k for k in range(pieces.shape[0]) if k != first]
    return lax.all_to_all(pieces, axes, 0, 0, axis_index_groups=[[first, *others]], tiled=True)


def per_device(strip_factors, sku_factors, probe, demand_weight):
    strips, skus = kernel_call(
        pack_kernel, (shape((8, 16, 128), BF16), shape((16, 1280), BF16)), 3, name="pack", room=63
    )(strip_factors, sku_factors.T, probe.T)
    panel = lax.all_gather(skus, "z_hi", axis=0)
    strips = from_first(strips, "z_lo", 3).reshape(128, 128)
    strips = jnp.broadcast_to(strips[None], (16, 128, 128))
    strips = lax.all_to_all(strips, ("y", "x"), 0, 0, tiled=True).reshape(2048, 128)
    panel = lax.all_gather(panel, "core", axis=0)
    unit, columns = kernel_call(
        prepare_kernel, (shape((2048, 64), BF16), shape((16, 2048), BF16)), 1, name="prepare"
    )(panel)
    total = kernel_call(
        image_kernel, shape((16, 32, 128)), 3, name="image", scratch=[pltpu.VMEM((128, 2048), BF16)]
    )(strips, unit, columns)
    total = lax.all_to_all(total, ("y", "x"), 0, 0, tiled=True)
    total = kernel_call(turn_kernel, shape((8, 4, 128)), 1, name="turn")(total)
    total = from_first(total, "z_lo", 3)
    image, gram = kernel_call(
        gram_kernel, (shape((16, 32)), shape((32, 2, 128))), 2, name="gram"
    )(total, demand_weight)
    gram = lax.all_to_all(gram, ("core", "y", "x"), 0, 0, tiled=True)
    gram = kernel_call(sum_kernel, shape((32, 2, 128)), 1, name="sum")(gram)
    gram = from_first(gram, ("z_hi", "z_lo"), 16)
    return kernel_call(basis_kernel, shape((16, 32)), 2, name="basis")(gram, image)


def solution(mesh):
    fine = Mesh(mesh.devices.reshape(SIZES), AXES)
    both = ROW + COL
    placed = (P(both, None), P(COL, ROW), P(COL, ROW), P(None, both))
    return jax.shard_map(
        per_device, mesh=fine, in_specs=placed, out_specs=P(None, both), check_vma=False
    )
```

```python
import jax
import jax.numpy as jnp
from jax import lax
from jax.experimental import pallas as pl
from jax.experimental.pallas import tpu as pltpu
from jax.sharding import Mesh
from jax.sharding import PartitionSpec as P

F32, BF16 = jnp.float32, jnp.bfloat16
AXES = ("z_hi", "core", "y", "x", "z_lo")
SIZES = (4, 2, 4, 4, 8)
ROW, COL = ("z_hi", "core"), ("y", "x", "z_lo")
VMEM = pl.BlockSpec(memory_space=pltpu.VMEM)
T_STEP, S_STEP = 1024, 512


def kernel_call(body, outs, count, scratch=(), name=None, room=40):
    return pl.pallas_call(
        body,
        out_shape=outs,
        in_specs=[VMEM] * count,
        out_specs=jax.tree.map(lambda _: VMEM, outs),
        scratch_shapes=list(scratch),
        name=name,
        compiler_params=pltpu.CompilerParams(vmem_limit_bytes=room * 2**20),
    )


def shape(dims, kind=F32):
    return jax.ShapeDtypeStruct(dims, kind)


def pack_kernel(strip_ref, sku_ref, probe_ref, strips_ref, skus_ref):
    wide = strip_ref[...].astype(F32)
    scale = lax.rsqrt(jnp.sum(wide * wide, axis=1, keepdims=True) + 1e-06)
    unit = wide * scale
    packed = jnp.concatenate([unit[:16], unit[16:]], axis=1).astype(BF16)
    strips_ref[...] = jnp.broadcast_to(packed[None], strips_ref.shape)
    sku = sku_ref[...].astype(F32)
    probe = probe_ref[...].astype(F32)
    factors = jnp.concatenate([sku[:, :1024], sku[:, 1024:]], axis=0)
    columns = jnp.concatenate([probe[:, 256 * m : 256 * (m + 1)] for m in range(8)], axis=0)
    skus_ref[...] = jnp.concatenate([factors, columns], axis=1).astype(BF16)


def prepare_kernel(panel_ref, unit_ref, probe_ref):
    factors, columns = [], []
    for z_hi in range(4):
        for core in range(2):
            piece = panel_ref[core, z_hi].astype(F32)
            factors.append(jnp.concatenate([piece[:8, :1024], piece[8:, :1024]], axis=1))
            columns.append(jnp.concatenate([piece[2 * m : 2 * m + 2, 1024:] for m in range(8)], axis=1))
    wide = jnp.concatenate(factors, axis=0)
    scale = lax.rsqrt(jnp.sum(wide * wide, axis=0, keepdims=True) + 1e-06)
    unit_ref[...] = (wide * scale).astype(BF16).T
    probe_ref[...] = jnp.concatenate(columns, axis=0).astype(BF16)


def image_kernel(strips_ref, unit_ref, probe_ref, out_ref, turned_ref):
    turned_ref[...] = strips_ref[...].T
    for half in range(2):
        for step in range(2048 // T_STEP):
            strip = turned_ref[64 * half : 64 * half + 64, T_STEP * step : T_STEP * (step + 1)]
            total = jnp.zeros((16, T_STEP), F32)
            for number in range(2048 // S_STEP):
                skus = slice(number * S_STEP, (number + 1) * S_STEP)
                corr = jnp.dot(unit_ref[skus, :], strip, preferred_element_type=F32)
                affinity = jnp.exp(corr).astype(BF16)
                total = total + jnp.dot(probe_ref[:, skus], affinity, preferred_element_type=F32)
            for k in range(T_STEP // 128):
                out_ref[step * (T_STEP // 128) + k, 16 * half : 16 * half + 16, :] = total[:, 128 * k : 128 * (k + 1)]


def turn_kernel(parts_ref, out_ref):
    total = parts_ref[0]
    for k in range(1, parts_ref.shape[0]):
        total = total + parts_ref[k]
    turned = total.T.reshape(8, 16, 32)
    out_ref[...] = jnp.concatenate([turned[:, 4 * b : 4 * b + 4, :] for b in range(4)], axis=2)


def gram_kernel(parts_ref, weight_ref, image_ref, gram_ref):
    total = parts_ref[0]
    for k in range(1, parts_ref.shape[0]):
        total = total + parts_ref[k]
    turned = jnp.concatenate([total[:, 32 * b : 32 * b + 32] for b in range(4)], axis=0).T
    image = jnp.concatenate([turned[:16], turned[16:]], axis=1)
    image_ref[...] = image
    gram = lax.dot_general(
        image * weight_ref[...], image, (((1,), (1,)), ((), ())),
        precision=lax.Precision.HIGHEST, preferred_element_type=F32,
    )
    packed = jnp.concatenate([gram[2 * b : 2 * b + 2] for b in range(8)], axis=1)
    gram_ref[...] = jnp.broadcast_to(packed[None], gram_ref.shape)


def sum_kernel(parts_ref, out_ref):
    total = parts_ref[0]
    for k in range(1, parts_ref.shape[0]):
        total = total + parts_ref[k]
    out_ref[...] = jnp.broadcast_to(total[None], out_ref.shape)


def basis_kernel(parts_ref, image_ref, out_ref):
    total = parts_ref[0]
    for k in range(1, parts_ref.shape[0]):
        total = total + parts_ref[k]
    gram = jnp.concatenate([total[:, 16 * b : 16 * b + 16] for b in range(8)], axis=0)
    left = image_ref[...]
    rows = lax.broadcasted_iota(jnp.int32, (16, 1), 0)
    for k in range(15):
        below = rows > k
        ratio = jnp.where(below, gram[:, k : k + 1] / gram[k : k + 1, k : k + 1], 0.0)
        left = left - ratio * left[k : k + 1, :]
        gram = gram - ratio * gram[k : k + 1, :]
    diagonal = rows == lax.broadcasted_iota(jnp.int32, (16, 16), 1)
    pivots = jnp.sum(jnp.where(diagonal, gram, 0.0), axis=1, keepdims=True)
    out_ref[...] = left / jnp.sqrt(pivots)


def from_first(pieces, axes, first):
    others = [k for k in range(pieces.shape[0]) if k != first]
    return lax.all_to_all(pieces, axes, 0, 0, axis_index_groups=[[first, *others]], tiled=True)


def per_device(strip_factors, sku_factors, probe, demand_weight):
    strips, skus = kernel_call(
        pack_kernel, (shape((8, 16, 128), BF16), shape((16, 1280), BF16)), 3, name="pack", room=63
    )(strip_factors, sku_factors.T, probe.T)
    panel = lax.all_gather(skus, "z_hi", axis=0)
    strips = from_first(strips, "z_lo", 4).reshape(128, 128)
    strips, panel = lax.optimization_barrier((strips, panel))
    strips = jnp.broadcast_to(strips[None], (16, 128, 128))
    strips = lax.all_to_all(strips, ("y", "x"), 0, 0, tiled=True).reshape(2048, 128)
    panel = lax.all_gather(panel, "core", axis=0)
    unit, columns = kernel_call(
        prepare_kernel, (shape((2048, 64), BF16), shape((16, 2048), BF16)), 1, name="prepare"
    )(panel)
    total = kernel_call(
        image_kernel, shape((16, 32, 128)), 3, name="image", scratch=[pltpu.VMEM((128, 2048), BF16)]
    )(strips, unit, columns)
    total = lax.all_to_all(total, ("y", "x"), 0, 0, tiled=True)
    total = kernel_call(turn_kernel, shape((8, 4, 128)), 1, name="turn")(total)
    total = from_first(total, "z_lo", 4)
    image, gram = kernel_call(
        gram_kernel, (shape((16, 32)), shape((32, 2, 128))), 2, name="gram"
    )(total, demand_weight)
    gram = lax.all_to_all(gram, ("core", "y", "x"), 0, 0, tiled=True)
    gram = kernel_call(sum_kernel, shape((32, 2, 128)), 1, name="sum")(gram)
    gram = from_first(gram, ("z_hi", "z_lo"), 16)
    return kernel_call(basis_kernel, shape((16, 32)), 2, name="basis")(gram, image)


def solution(mesh):
    fine = Mesh(mesh.devices.reshape(SIZES), AXES)
    both = ROW + COL
    placed = (P(both, None), P(COL, ROW), P(COL, ROW), P(None, both))
    return jax.shard_map(
        per_device, mesh=fine, in_specs=placed, out_specs=P(None, both), check_vma=False
    )
```

```python
import jax
import jax.numpy as jnp
from jax import lax
from jax.experimental import pallas as pl
from jax.experimental.pallas import tpu as pltpu
from jax.sharding import Mesh
from jax.sharding import PartitionSpec as P

F32, BF16 = jnp.float32, jnp.bfloat16
AXES = ("z_hi", "core", "y", "x", "z_lo")
SIZES = (4, 2, 4, 4, 8)
ROW, COL = ("z_hi", "core"), ("y", "x", "z_lo")
VMEM = pl.BlockSpec(memory_space=pltpu.VMEM)
SMEM = pl.BlockSpec(memory_space=pltpu.SMEM)
S_STEP = 1024


def kernel_call(body, outs, count, scratch=(), name=None, room=40, smem=0):
    return pl.pallas_call(
        body,
        out_shape=outs,
        in_specs=[SMEM] * smem + [VMEM] * (count - smem),
        out_specs=jax.tree.map(lambda _: VMEM, outs),
        scratch_shapes=list(scratch),
        name=name,
        compiler_params=pltpu.CompilerParams(vmem_limit_bytes=room * 2**20),
    )


def shape(dims, kind=F32):
    return jax.ShapeDtypeStruct(dims, kind)


def pack_kernel(strip_ref, sku_ref, probe_ref, strips_ref, skus_ref):
    wide = strip_ref[...].astype(F32)
    scale = lax.rsqrt(jnp.sum(wide * wide, axis=1, keepdims=True) + 1e-06)
    unit = wide * scale
    packed = jnp.concatenate([unit[:16], unit[16:]], axis=1).astype(BF16)
    strips_ref[...] = jnp.broadcast_to(packed[None], strips_ref.shape)
    sku = sku_ref[...].astype(F32)
    probe = probe_ref[...].astype(F32)
    factors = jnp.concatenate([sku[:, :1024], sku[:, 1024:]], axis=0)
    columns = jnp.concatenate([probe[:, 256 * m : 256 * (m + 1)] for m in range(8)], axis=0)
    skus_ref[...] = jnp.concatenate([factors, columns], axis=1).astype(BF16)


def prepare_kernel(panel_ref, unit_ref, probe_ref):
    factors, columns = [], []
    for z_hi in range(4):
        for core in range(2):
            piece = panel_ref[core, z_hi].astype(F32)
            factors.append(jnp.concatenate([piece[:8, :1024], piece[8:, :1024]], axis=1))
            columns.append(jnp.concatenate([piece[2 * m : 2 * m + 2, 1024:] for m in range(8)], axis=1))
    wide = jnp.concatenate(factors, axis=0)
    scale = lax.rsqrt(jnp.sum(wide * wide, axis=0, keepdims=True) + 1e-06)
    unit_ref[...] = (wide * scale).astype(BF16).T
    probe_ref[...] = jnp.concatenate(columns, axis=0).astype(BF16)


def add_image(strips, unit_ref, probe_ref, half):
    strip = strips[64 * half : 64 * half + 64, :]
    total = jnp.zeros((16, 512), F32)
    for number in range(2048 // S_STEP):
        skus = slice(number * S_STEP, (number + 1) * S_STEP)
        corr = jnp.dot(unit_ref[skus, :], strip, preferred_element_type=F32)
        affinity = jnp.exp(corr).astype(BF16)
        total = total + jnp.dot(probe_ref[:, skus], affinity, preferred_element_type=F32)
    return total


def own_kernel(strips_ref, unit_ref, probe_ref, out_ref):
    turned = strips_ref[...].T
    for half in range(2):
        total = add_image(turned, unit_ref, probe_ref, half)
        for k in range(4):
            out_ref[k, 16 * half : 16 * half + 16, :] = total[:, 128 * k : 128 * (k + 1)]


def image_kernel(y_ref, strips_ref, unit_ref, probe_ref, own_ref, out_ref):
    y = y_ref[0]
    out_ref[pl.ds(4 * y, 4)] = own_ref[...]
    for other in range(1, 4):
        place = lax.rem(y + other, 4)
        turned = strips_ref[pl.ds(pl.multiple_of(512 * place, 512), 512), :].T
        for half in range(2):
            total = add_image(turned, unit_ref, probe_ref, half)
            for k in range(4):
                out_ref[4 * place + k, 16 * half : 16 * half + 16, :] = total[:, 128 * k : 128 * (k + 1)]


def turn_kernel(parts_ref, out_ref):
    total = parts_ref[0]
    for k in range(1, parts_ref.shape[0]):
        total = total + parts_ref[k]
    turned = total.T.reshape(8, 16, 32)
    out_ref[...] = jnp.concatenate([turned[:, 4 * b : 4 * b + 4, :] for b in range(4)], axis=2)


def gram_kernel(parts_ref, weight_ref, image_ref, gram_ref):
    total = parts_ref[0]
    for k in range(1, parts_ref.shape[0]):
        total = total + parts_ref[k]
    turned = jnp.concatenate([total[:, 32 * b : 32 * b + 32] for b in range(4)], axis=0).T
    image = jnp.concatenate([turned[:16], turned[16:]], axis=1)
    image_ref[...] = image
    gram = lax.dot_general(
        image * weight_ref[...], image, (((1,), (1,)), ((), ())),
        precision=lax.Precision.HIGHEST, preferred_element_type=F32,
    )
    packed = jnp.concatenate([gram[2 * b : 2 * b + 2] for b in range(8)], axis=1)
    gram_ref[...] = jnp.broadcast_to(packed[None], gram_ref.shape)


def sum_kernel(parts_ref, out_ref):
    total = parts_ref[0]
    for k in range(1, parts_ref.shape[0]):
        total = total + parts_ref[k]
    out_ref[...] = jnp.broadcast_to(total[None], out_ref.shape)


def basis_kernel(parts_ref, image_ref, out_ref):
    total = parts_ref[0]
    for k in range(1, parts_ref.shape[0]):
        total = total + parts_ref[k]
    gram = jnp.concatenate([total[:, 16 * b : 16 * b + 16] for b in range(8)], axis=0)
    left = image_ref[...]
    rows = lax.broadcasted_iota(jnp.int32, (16, 1), 0)
    for k in range(15):
        below = rows > k
        ratio = jnp.where(below, gram[:, k : k + 1] / gram[k : k + 1, k : k + 1], 0.0)
        left = left - ratio * left[k : k + 1, :]
        gram = gram - ratio * gram[k : k + 1, :]
    diagonal = rows == lax.broadcasted_iota(jnp.int32, (16, 16), 1)
    pivots = jnp.sum(jnp.where(diagonal, gram, 0.0), axis=1, keepdims=True)
    out_ref[...] = left / jnp.sqrt(pivots)


Z_LO_ORDER = [4, 0, 1, 2, 3, 5, 6, 7]
X_Z_LO_ORDER = [8 * x + z for x in range(4) for z in Z_LO_ORDER]
Z_ORDER = [16, 0] + [z for k in range(1, 16) for z in (32 - k, k)]


def exchange(pieces, axes, order=None):
    groups = None if order is None else [order]
    return lax.all_to_all(pieces, axes, 0, 0, axis_index_groups=groups, tiled=True)


def per_device(strip_factors, sku_factors, probe, demand_weight):
    strips, skus = kernel_call(
        pack_kernel, (shape((32, 16, 128), BF16), shape((16, 1280), BF16)), 3, name="pack", room=63
    )(strip_factors, sku_factors.T, probe.T)
    panel = lax.all_gather(skus, "z_hi", axis=0)
    strips = exchange(strips, ("x", "z_lo"), X_Z_LO_ORDER).reshape(512, 128)
    strips, panel = lax.optimization_barrier((strips, panel))
    own = strips
    strips = exchange(jnp.broadcast_to(strips[None], (4, 512, 128)), "y").reshape(2048, 128)
    panel = lax.all_gather(panel, "core", axis=0)
    unit, columns = kernel_call(
        prepare_kernel, (shape((2048, 64), BF16), shape((16, 2048), BF16)), 1, name="prepare"
    )(panel)
    total = kernel_call(own_kernel, shape((4, 32, 128)), 3, name="own")(own, unit, columns)
    place = jnp.full((1,), lax.axis_index("y"), jnp.int32)
    total = kernel_call(image_kernel, shape((16, 32, 128)), 5, smem=1, name="image")(
        place, strips, unit, columns, total
    )
    total = exchange(total, ("y", "x"))
    total = kernel_call(turn_kernel, shape((8, 4, 128)), 1, name="turn")(total)
    total = exchange(total, "z_lo", Z_LO_ORDER)
    image, gram = kernel_call(
        gram_kernel, (shape((16, 32)), shape((32, 2, 128))), 2, name="gram"
    )(total, demand_weight)
    gram = exchange(gram, ("core", "y", "x"))
    gram = kernel_call(sum_kernel, shape((32, 2, 128)), 1, name="sum")(gram)
    gram = exchange(gram, ("z_hi", "z_lo"), Z_ORDER)
    return kernel_call(basis_kernel, shape((16, 32)), 2, name="basis")(gram, image)


def solution(mesh):
    fine = Mesh(mesh.devices.reshape(SIZES), AXES)
    both = ROW + COL
    placed = (P(both, None), P(COL, ROW), P(COL, ROW), P(None, both))
    return jax.shard_map(
        per_device, mesh=fine, in_specs=placed, out_specs=P(None, both), check_vma=False
    )
```

```python
import jax
import jax.numpy as jnp
from jax import lax
from jax.experimental import pallas as pl
from jax.experimental.pallas import tpu as pltpu
from jax.sharding import Mesh
from jax.sharding import PartitionSpec as P

F32, BF16 = jnp.float32, jnp.bfloat16
AXES = ("z_hi", "core", "y", "x", "z_lo")
SIZES = (4, 2, 4, 4, 8)
ROW, COL = ("z_hi", "core"), ("y", "x", "z_lo")
VMEM = pl.BlockSpec(memory_space=pltpu.VMEM)
SMEM = pl.BlockSpec(memory_space=pltpu.SMEM)
S_STEP = 1024


def kernel_call(body, outs, count, scratch=(), name=None, room=40, smem=0):
    return pl.pallas_call(
        body,
        out_shape=outs,
        in_specs=[SMEM] * smem + [VMEM] * (count - smem),
        out_specs=jax.tree.map(lambda _: VMEM, outs),
        scratch_shapes=list(scratch),
        name=name,
        compiler_params=pltpu.CompilerParams(vmem_limit_bytes=room * 2**20),
    )


def shape(dims, kind=F32):
    return jax.ShapeDtypeStruct(dims, kind)


def pack_kernel(strip_ref, sku_ref, probe_ref, strips_ref, skus_ref):
    wide = strip_ref[...].astype(F32)
    scale = lax.rsqrt(jnp.sum(wide * wide, axis=1, keepdims=True) + 1e-06)
    unit = wide * scale
    packed = jnp.concatenate([unit[:16], unit[16:]], axis=1).astype(BF16)
    strips_ref[...] = jnp.broadcast_to(packed[None], strips_ref.shape)
    sku = sku_ref[...].astype(F32)
    probe = probe_ref[...].astype(F32)
    factors = jnp.concatenate([sku[:, :1024], sku[:, 1024:]], axis=0)
    columns = jnp.concatenate([probe[:, 256 * m : 256 * (m + 1)] for m in range(8)], axis=0)
    skus_ref[...] = jnp.concatenate([factors, columns], axis=1).astype(BF16)


def prepare_kernel(panel_ref, unit_ref, probe_ref):
    factors, columns = [], []
    for z_hi in range(4):
        for core in range(2):
            piece = panel_ref[core, z_hi].astype(F32)
            factors.append(jnp.concatenate([piece[:8, :1024], piece[8:, :1024]], axis=1))
            columns.append(jnp.concatenate([piece[2 * m : 2 * m + 2, 1024:] for m in range(8)], axis=1))
    wide = jnp.concatenate(factors, axis=0)
    scale = lax.rsqrt(jnp.sum(wide * wide, axis=0, keepdims=True) + 1e-06)
    unit_ref[...] = (wide * scale).astype(BF16).T
    probe_ref[...] = jnp.concatenate(columns, axis=0).astype(BF16)


def add_image(strips, unit_ref, probe_ref, half):
    strip = strips[64 * half : 64 * half + 64, :]
    total = jnp.zeros((16, 512), F32)
    for number in range(2048 // S_STEP):
        skus = slice(number * S_STEP, (number + 1) * S_STEP)
        corr = jnp.dot(unit_ref[skus, :], strip, preferred_element_type=F32)
        affinity = jnp.exp(corr).astype(BF16)
        total = total + jnp.dot(probe_ref[:, skus], affinity, preferred_element_type=F32)
    return total


def own_kernel(strips_ref, unit_ref, probe_ref, out_ref):
    turned = strips_ref[...].T
    for half in range(2):
        total = add_image(turned, unit_ref, probe_ref, half)
        for k in range(4):
            out_ref[k, 16 * half : 16 * half + 16, :] = total[:, 128 * k : 128 * (k + 1)]


def image_kernel(y_ref, strips_ref, unit_ref, probe_ref, own_ref, out_ref):
    y = y_ref[0]
    out_ref[pl.ds(4 * y, 4)] = own_ref[...]
    for other in range(1, 4):
        place = lax.rem(y + other, 4)
        turned = strips_ref[pl.ds(pl.multiple_of(512 * place, 512), 512), :].T
        for half in range(2):
            total = add_image(turned, unit_ref, probe_ref, half)
            for k in range(4):
                out_ref[4 * place + k, 16 * half : 16 * half + 16, :] = total[:, 128 * k : 128 * (k + 1)]


def turn_kernel(parts_ref, out_ref):
    total = parts_ref[0]
    for k in range(1, parts_ref.shape[0]):
        total = total + parts_ref[k]
    turned = total.T.reshape(8, 16, 32)
    out_ref[...] = jnp.concatenate([turned[:, 4 * b : 4 * b + 4, :] for b in range(4)], axis=2)


def gram_kernel(parts_ref, weight_ref, image_ref, gram_ref):
    total = parts_ref[0]
    for k in range(1, parts_ref.shape[0]):
        total = total + parts_ref[k]
    turned = jnp.concatenate([total[:, 32 * b : 32 * b + 32] for b in range(4)], axis=0).T
    image = jnp.concatenate([turned[:16], turned[16:]], axis=1)
    image_ref[...] = image
    gram = lax.dot_general(
        image * weight_ref[...], image, (((1,), (1,)), ((), ())),
        precision=lax.Precision.HIGHEST, preferred_element_type=F32,
    )
    packed = jnp.concatenate([gram[2 * b : 2 * b + 2] for b in range(8)], axis=1)
    gram_ref[...] = jnp.broadcast_to(packed[None], gram_ref.shape)


def sum_kernel(parts_ref, out_ref):
    total = parts_ref[0]
    for k in range(1, parts_ref.shape[0]):
        total = total + parts_ref[k]
    out_ref[...] = jnp.broadcast_to(total[None], out_ref.shape)


def basis_kernel(parts_ref, image_ref, out_ref):
    total = parts_ref[0]
    for k in range(1, parts_ref.shape[0]):
        total = total + parts_ref[k]
    gram = jnp.concatenate([total[:, 16 * b : 16 * b + 16] for b in range(8)], axis=0)
    left = image_ref[...]
    rows = lax.broadcasted_iota(jnp.int32, (16, 1), 0)
    for k in range(15):
        below = rows > k
        ratio = jnp.where(below, gram[:, k : k + 1] / gram[k : k + 1, k : k + 1], 0.0)
        left = left - ratio * left[k : k + 1, :]
        gram = gram - ratio * gram[k : k + 1, :]
    diagonal = rows == lax.broadcasted_iota(jnp.int32, (16, 16), 1)
    pivots = jnp.sum(jnp.where(diagonal, gram, 0.0), axis=1, keepdims=True)
    out_ref[...] = left / jnp.sqrt(pivots)


Z_LO_ORDER = [3, 0, 1, 2, 4, 5, 6, 7]
X_Z_LO_ORDER = [8 * x + z for x in range(4) for z in Z_LO_ORDER]
Z_ORDER = [16, 0] + [z for k in range(1, 16) for z in (32 - k, k)]


def exchange(pieces, axes, order=None):
    groups = None if order is None else [order]
    return lax.all_to_all(pieces, axes, 0, 0, axis_index_groups=groups, tiled=True)


def per_device(strip_factors, sku_factors, probe, demand_weight):
    strips, skus = kernel_call(
        pack_kernel, (shape((32, 16, 128), BF16), shape((16, 1280), BF16)), 3, name="pack", room=63
    )(strip_factors, sku_factors.T, probe.T)
    panel = lax.all_gather(skus, "z_hi", axis=0)
    strips = exchange(strips, ("x", "z_lo"), X_Z_LO_ORDER).reshape(512, 128)
    strips, panel = lax.optimization_barrier((strips, panel))
    own = strips
    strips = exchange(jnp.broadcast_to(strips[None], (4, 512, 128)), "y").reshape(2048, 128)
    panel = lax.all_gather(panel, "core", axis=0)
    unit, columns = kernel_call(
        prepare_kernel, (shape((2048, 64), BF16), shape((16, 2048), BF16)), 1, name="prepare"
    )(panel)
    total = kernel_call(own_kernel, shape((4, 32, 128)), 3, name="own")(own, unit, columns)
    place = jnp.full((1,), lax.axis_index("y"), jnp.int32)
    total = kernel_call(image_kernel, shape((16, 32, 128)), 5, smem=1, name="image")(
        place, strips, unit, columns, total
    )
    total = exchange(total, ("y", "x"))
    total = kernel_call(turn_kernel, shape((8, 4, 128)), 1, name="turn")(total)
    total = exchange(total, "z_lo", Z_LO_ORDER)
    image, gram = kernel_call(
        gram_kernel, (shape((16, 32)), shape((32, 2, 128))), 2, name="gram"
    )(total, demand_weight)
    gram = exchange(gram, ("core", "y", "x"))
    gram = kernel_call(sum_kernel, shape((32, 2, 128)), 1, name="sum")(gram)
    gram = exchange(gram, ("z_hi", "z_lo"), Z_ORDER)
    return kernel_call(basis_kernel, shape((16, 32)), 2, name="basis")(gram, image)


def solution(mesh):
    fine = Mesh(mesh.devices.reshape(SIZES), AXES)
    both = ROW + COL
    placed = (P(both, None), P(COL, ROW), P(COL, ROW), P(None, both))
    return jax.shard_map(
        per_device, mesh=fine, in_specs=placed, out_specs=P(None, both), check_vma=False
    )
```
